32 devices in a mesh: band: 16 (over z, y, x), chan: 2 (over core).
Axes of the slice: x: 2, y: 2, z: 4, core: 2. Of those that a mesh axis runs over, the one named last changes fastest.
Arguments:
- latent: bfloat16 [384, 48, 1440], P(None, 'band'), may hold values from -6 to 6
- decoder_weight: bfloat16 [42, 384], P('chan'), may hold values from -0.3125 to 0.3125
- target: bfloat16 [42, 48, 1440], P('chan', 'band'), may hold values from -6 to 6
Outputs:
- grad_latent: bfloat16 [384, 48, 1440], P('chan', 'band')
- grad_weight: float32 [42, 384], P('chan')
- loss_spectrum: float32 [42, 721], P('chan')
The draws below stay inside these ranges and needn't reach their ends.
All inputs are finite; a program needn't handle non-finite values.
Results may differ from the reference program's by a relative error of at most 0.0077.
Values may be sent and summed in bfloat16 or wider, within the bound.
A program may use at most 128 MiB of HBM per device.

```python
import math
import jax
import jax.numpy as jnp
from jax import lax

NLON = 1440
TRUNC = 720
MPAD = 768
KL = 384
CH = 42
NLAT = 48
NL = 721
NLP = 768


def block_levels(stream_key, shape, shards, smallest, largest):
    def one(dim, parts):
        draws = jax.random.uniform(jax.random.fold_in(jax.random.fold_in(stream_key, 6), dim), (parts,), jnp.float32, smallest / len(shards), largest / len(shards))
        return jnp.repeat(jnp.exp(draws), shape[dim] // parts).reshape((-1,) + (1,) * (len(shape) - dim - 1))

    factor_of = one(*shards[0])
    for cut in shards[1:]:
        factor_of = factor_of * one(*cut)
    return factor_of


def noise(rng, dims, deviation, bound, cuts=(), kind=jnp.bfloat16):
    loudness = block_levels(rng, dims, cuts, -0.22, 0.18) if cuts else 1.0
    drawn = jax.random.normal(rng, dims, jnp.float32) * deviation * loudness
    return jnp.minimum(jnp.maximum(drawn, -bound), bound).astype(kind)


def setup_inputs(seed: int = 0) -> dict:
    key_list = jax.random.split(jax.random.key(seed), 4)
    return {
        "latent": noise(key_list[0], (KL, NLAT, NLON), 1.0, 6.0, ((1, 16),)),
        "decoder_weight": noise(key_list[1], (CH, KL), KL ** -0.5, 0.3125, ((0, 2),)),
        "target": noise(key_list[2], (CH, NLAT, NLON), 1.0, 6.0, ((0, 2), (1, 16))),
    }


def fourier_table(order_ids):
    longitude = jnp.arange(NLON).astype(jnp.int32)
    phase_index = longitude[:, None] * order_ids[None, :] % NLON
    angles = 2.0 * math.pi / NLON * phase_index.astype(jnp.float32)
    in_range = (order_ids <= TRUNC)[None, :]
    norm_scale = 1.0 / math.sqrt(NLON)
    cosines = jnp.where(in_range, jnp.cos(angles) * norm_scale, 0.0)
    negsines = jnp.where(in_range, -jnp.sin(angles) * norm_scale, 0.0)
    return jnp.stack([cosines, negsines], axis=1).astype(jnp.bfloat16)

def legendre_table(order_ids, lat_count, row_total, cutoff):
    lat_index = jnp.arange(lat_count).astype(jnp.float32)
    colatitude = math.pi * (lat_index + 0.5) / lat_count
    cosines = jnp.cos(colatitude)
    colat_sin = jnp.sin(colatitude)
    weights = math.sqrt(math.pi / lat_count) * colat_sin
    order_float = order_ids.astype(jnp.float32)[:, None]
    log_start = 0.5 * jnp.log(order_float + 0.5) + lax.lgamma(order_float + 0.5) - lax.lgamma(order_float + 1.0) - 0.5 * math.log(math.pi) + order_float * jnp.log(colat_sin)[None, :]
    zero_rows = jnp.zeros((order_ids.shape[0], lat_count), jnp.float32)

    def advance(carried, offset):
        before, current, log_scale = carried
        scaled = current * jnp.exp(log_scale)
        degree = order_float + offset.astype(jnp.float32) + 1.0
        previous_degree = degree - 1.0
        factor = jnp.sqrt((4.0 * degree * degree - 1.0) / (degree * degree - order_float * order_float))
        back_factor = jnp.sqrt(jnp.maximum(previous_degree * previous_degree - order_float * order_float, 0.0) / (4.0 * previous_degree * previous_degree - 1.0))
        following = factor * (cosines[None, :] * current - back_factor * before)
        magnitude = jnp.sqrt(current * current + following * following)
        return ((current / magnitude, following / magnitude, log_scale + jnp.log(magnitude)), scaled)
    initial = (zero_rows, zero_rows + 1.0, log_start)
    _, stacked = lax.scan(advance, initial, jnp.arange(row_total).astype(jnp.int32), unroll=4)
    stacked = jnp.transpose(stacked, (1, 0, 2))
    degrees = order_ids[:, None] + jnp.arange(row_total).astype(jnp.int32)[None, :]
    inside = (degrees <= cutoff)[:, :, None]
    return jnp.where(inside, stacked * weights[None, None, :], 0.0).astype(jnp.bfloat16)

def spectral_terms(power_pred, power_true, cross_power):
    first_power = power_pred + 1.0
    second_power = power_true + 1.0
    first_root = jnp.sqrt(first_power)
    second_root = jnp.sqrt(second_power)
    joint_root = first_root * second_root
    coherence = cross_power / joint_root
    combined = first_power + second_power
    loss_terms = jnp.square(first_root - second_root) + combined * (1.0 - coherence)
    d_power = 2.0 - second_root / first_root - coherence + combined * cross_power / (2.0 * first_power * joint_root)
    d_cross = -combined / joint_root
    return (loss_terms, d_power, d_cross)

def reference(latent, decoder_weight, target):
    cell_count = NLAT * NLON
    flat_latent = latent.reshape(KL, cell_count)
    predicted = jnp.dot(decoder_weight, flat_latent, preferred_element_type=jnp.float32).astype(jnp.bfloat16)
    fields = jnp.stack([predicted.reshape(CH, NLAT, NLON), target])
    order_all = jnp.arange(MPAD).astype(jnp.int32)
    harmonic_basis = fourier_table(order_all)
    fourier_modes = jnp.einsum('fclk,kqm->mlfcq', fields.astype(jnp.float32), harmonic_basis.astype(jnp.float32))
    fourier_modes = fourier_modes.astype(jnp.bfloat16).reshape(MPAD // 32, 32, NLAT, 4 * CH)
    order_blocks = order_all.reshape(MPAD // 32, 32)

    def analyse(packed):
        block_orders, fourier_block_slice = packed
        tables = legendre_table(block_orders, NLAT, NLP, TRUNC)
        return jnp.einsum('mtj,mjc->mtc', tables.astype(jnp.float32), fourier_block_slice.astype(jnp.float32))
    coefficients = lax.map(analyse, (order_blocks, fourier_modes)).reshape(MPAD, NLP, 2, CH, 2)
    pred_coef = coefficients[:, :, 0]
    true_coef = coefficients[:, :, 1]
    spectra_local = jnp.concatenate([lax.optimization_barrier(jnp.sum(pred_coef * pred_coef, axis=-1)), lax.optimization_barrier(jnp.sum(true_coef * true_coef, axis=-1)), lax.optimization_barrier(jnp.sum(pred_coef * true_coef, axis=-1))], axis=-1)
    degrees = (order_all[:, None] + jnp.arange(NLP).astype(jnp.int32)[None, :]).reshape(-1)
    totals = jnp.zeros((MPAD + NLP, 3 * CH), jnp.float32).at[degrees].add(spectra_local.reshape(-1, 3 * CH))[:NL]
    loss_terms, d_power, d_cross = spectral_terms(totals[:, :CH], totals[:, CH:2 * CH], totals[:, 2 * CH:])
    derivative = jnp.concatenate([d_power, d_cross], axis=1)
    padded = jnp.concatenate([derivative, jnp.zeros((MPAD + NLP - NL, 2 * CH), jnp.float32)], axis=0)
    aligned = padded[degrees].reshape(MPAD, NLP, 2 * CH)
    gradient = 2.0 * aligned[:, :, :CH, None] * pred_coef + aligned[:, :, CH:, None] * true_coef
    gradient = gradient.astype(jnp.bfloat16).reshape(MPAD // 32, 32, NLP, 2 * CH)

    def synthesise(packed):
        block_orders, block_gradient = packed
        tables = legendre_table(block_orders, NLAT, NLP, TRUNC)
        summed = jnp.einsum('mtj,mtc->mjc', tables.astype(jnp.float32), block_gradient.astype(jnp.float32))
        return summed.astype(jnp.bfloat16)
    inverse_transform = lax.map(synthesise, (order_blocks, gradient)).reshape(MPAD, NLAT, CH, 2)
    upstream_gradient = jnp.einsum('tjxv,bvt->xjb', inverse_transform.astype(jnp.float32), harmonic_basis.astype(jnp.float32))
    flat_cot = upstream_gradient.astype(jnp.bfloat16).reshape(CH, cell_count)
    grad_weight = lax.dot_general(flat_cot, flat_latent, (((1,), (1,)), ((), ())), preferred_element_type=jnp.float32) / math.sqrt(cell_count)
    latent_sum = lax.dot_general(decoder_weight, flat_cot, (((0,), (0,)), ((), ())), preferred_element_type=jnp.float32)
    grad_latent = latent_sum.astype(jnp.bfloat16).reshape(KL, NLAT, NLON)
    return (grad_latent, grad_weight, loss_terms.T)
```

```python
import functools
import math

import jax
import jax.numpy as jnp
from jax import lax
from jax.experimental import pallas as pl
from jax.experimental.pallas import tpu as pltpu
from jax.sharding import PartitionSpec as P

NLON = 1440
TRUNC = 720
MPAD = 768
NL = 721
NLP = 768


def fourier_table(order_ids):
    longitude = jnp.arange(NLON)
    phase_index = longitude[:, None] * order_ids[None, :] % NLON
    angles = 2.0 * math.pi / NLON * phase_index.astype(jnp.float32)
    in_range = (order_ids <= TRUNC)[None, :]
    norm_scale = 1.0 / math.sqrt(NLON)
    cosines = jnp.where(in_range, jnp.cos(angles) * norm_scale, 0.0)
    negsines = jnp.where(in_range, -jnp.sin(angles) * norm_scale, 0.0)
    return jnp.stack([cosines, negsines], axis=1).astype(jnp.bfloat16)


def legendre_kernel(cutoff, step_rows, order_ref, start_ref, cos_ref, weight_ref, out_ref, before_ref, current_ref, scale_ref):
    step = pl.program_id(0)

    @pl.when(step == 0)
    def _():
        before_ref[...] = jnp.zeros_like(before_ref)
        current_ref[...] = jnp.ones_like(current_ref)
        scale_ref[...] = start_ref[...]

    order = order_ref[...]
    cosines = cos_ref[...]
    weights = weight_ref[...]
    squared = order * order
    before = before_ref[...]
    current = current_ref[...]
    log_scale = scale_ref[...]
    for row in range(step_rows):
        previous = order + (step * step_rows + row).astype(jnp.float32)
        degree = previous + 1.0
        value = current * jnp.exp(log_scale) * weights
        out_ref[row] = jnp.where(previous <= cutoff, value, 0.0).astype(out_ref.dtype)
        factor = jnp.sqrt((4.0 * degree * degree - 1.0) / (degree * degree - squared))
        back_factor = jnp.sqrt(
            jnp.maximum(previous * previous - squared, 1e-30)
            / jnp.abs(4.0 * previous * previous - 1.0)
        )
        following = factor * (cosines * current - back_factor * before)
        length = current * current + following * following
        inverse = lax.rsqrt(length)
        before = current * inverse
        current = following * inverse
        log_scale = log_scale + 0.5 * jnp.log(length)
    before_ref[...] = before
    current_ref[...] = current
    scale_ref[...] = log_scale


def legendre_rows(order_ids, lat_count, row_total, cutoff):
    lat_index = jnp.arange(lat_count).astype(jnp.float32)
    colatitude = math.pi * (lat_index + 0.5) / lat_count
    cosines = jnp.cos(colatitude)
    colat_sin = jnp.sin(colatitude)
    weights = math.sqrt(math.pi / lat_count) * colat_sin
    order_float = order_ids.astype(jnp.float32)[:, None]
    log_start = (
        0.5 * jnp.log(order_float + 0.5)
        + lax.lgamma(order_float + 0.5)
        - lax.lgamma(order_float + 1.0)
        - 0.5 * math.log(math.pi)
        + order_float * jnp.log(colat_sin)[None, :]
    )
    shape = log_start.shape
    operands = [
        jnp.broadcast_to(order_float, shape),
        log_start,
        jnp.broadcast_to(cosines[None, :], shape),
        jnp.broadcast_to(weights[None, :], shape),
    ]
    step_rows = 16
    return pl.pallas_call(
        functools.partial(legendre_kernel, float(cutoff), step_rows),
        grid=(row_total // step_rows,),
        out_shape=jax.ShapeDtypeStruct((row_total,) + shape, jnp.bfloat16),
        in_specs=[pl.BlockSpec(shape, lambda i: (0, 0))] * 4,
        out_specs=pl.BlockSpec((step_rows,) + shape, lambda i: (i, 0, 0)),
        scratch_shapes=[pltpu.VMEM(shape, jnp.float32)] * 3,
        name="legendre",
    )(*operands)


def analyse_kernel(rows, width, table_ref, columns_ref, out_ref):
    slot = pl.program_id(0)

    @pl.when(slot == 0)
    def _():
        out_ref[...] = jnp.zeros_like(out_ref)

    coef = jnp.dot(columns_ref[0], table_ref[0], preferred_element_type=jnp.float32)
    p0, p1, t0, t1 = (coef[i * rows : (i + 1) * rows] for i in range(4))
    spectra = jnp.concatenate([p0 * p0 + p1 * p1, t0 * t0 + t1 * t1, p0 * t0 + p1 * t1], axis=0)
    spare = jnp.zeros((3 * rows, width - spectra.shape[1]), jnp.float32)
    out_ref[...] += pltpu.roll(jnp.concatenate([spectra, spare], axis=1), slot, 1)


def synthesise_kernel(rows, width, table_ref, columns_ref, derivative_ref, out_ref):
    slot = pl.program_id(0)
    table = table_ref[0]
    coef = jnp.dot(columns_ref[0], table, preferred_element_type=jnp.float32)
    p0, p1, t0, t1 = (coef[i * rows : (i + 1) * rows] for i in range(4))
    aligned = pltpu.roll(derivative_ref[...], width - slot, 1)[:, : table.shape[1]]
    d_power, d_cross = 2.0 * aligned[:rows], aligned[rows:]
    gradient = jnp.concatenate([d_power * p0 + d_cross * t0, d_power * p1 + d_cross * t1], axis=0)
    out_ref[0] = lax.dot_general(
        gradient.astype(jnp.bfloat16),
        table,
        (((1,), (1,)), ((), ())),
        preferred_element_type=jnp.float32,
    ).astype(out_ref.dtype)


def spectral_terms(power_pred, power_true, cross_power):
    first_power = power_pred + 1.0
    second_power = power_true + 1.0
    first_root = jnp.sqrt(first_power)
    second_root = jnp.sqrt(second_power)
    joint_root = first_root * second_root
    coherence = cross_power / joint_root
    combined = first_power + second_power
    loss_terms = jnp.square(first_root - second_root) + combined * (1.0 - coherence)
    d_power = (
        2.0
        - second_root / first_root
        - coherence
        + combined * cross_power / (2.0 * first_power * joint_root)
    )
    d_cross = -combined / joint_root
    return (loss_terms, d_power, d_cross)


def local(latent, decoder_weight, target):
    bands = lax.axis_size("band")
    band_index = lax.axis_index("band")
    band_partition = MPAD // bands
    latitude_rows = target.shape[1]
    channels = target.shape[0]
    latent_width = latent.shape[0]
    cell_count = latitude_rows * NLON
    slot_ids = jnp.arange(MPAD)
    resident_orders = lax.dynamic_slice_in_dim(
        slot_ids, band_index * band_partition, band_partition, 0
    )
    flat_latent = latent.reshape(latent_width, cell_count)
    predicted = jnp.dot(decoder_weight, flat_latent, preferred_element_type=jnp.float32).astype(
        jnp.bfloat16
    )
    fields = jnp.stack([predicted.reshape(channels, latitude_rows, NLON), target])
    harmonic_basis = fourier_table(slot_ids)
    fourier_modes = jnp.einsum(
        "fclk,kqm->mfqcl", fields, harmonic_basis, preferred_element_type=jnp.float32
    )
    fourier_modes = fourier_modes.astype(jnp.bfloat16).reshape(MPAD, 4 * channels, latitude_rows)
    columns = lax.all_to_all(fourier_modes, "band", split_axis=0, concat_axis=2, tiled=True)
    lat_count = columns.shape[2]
    tables = legendre_rows(resident_orders, lat_count, NLP, TRUNC).transpose(1, 2, 0)
    rows = -(-channels // 8) * 8
    width = NLP + -(-band_partition // 128) * 128
    padded_columns = jnp.pad(
        columns.reshape(band_partition, 4, channels, lat_count),
        ((0, 0), (0, 0), (0, rows - channels), (0, 0)),
    ).reshape(band_partition, 4 * rows, lat_count)
    table_spec = pl.BlockSpec((1, lat_count, NLP), lambda i: (i, 0, 0))
    column_spec = pl.BlockSpec((1, 4 * rows, lat_count), lambda i: (i, 0, 0))
    first_order = band_index * band_partition
    spectra_local = pl.pallas_call(
        functools.partial(analyse_kernel, rows, width),
        grid=(band_partition,),
        out_shape=jax.ShapeDtypeStruct((3 * rows, width), jnp.float32),
        in_specs=[table_spec, column_spec],
        out_specs=pl.BlockSpec((3 * rows, width), lambda i: (0, 0)),
        name="analyse",
    )(tables, padded_columns)
    by_degree = lax.dynamic_update_slice(
        jnp.zeros((3 * rows, MPAD + width), jnp.float32), spectra_local, (0, first_order)
    )
    by_degree = by_degree.reshape(3, rows, MPAD + width)[:, :channels, :NL]
    totals = lax.psum(by_degree.reshape(3 * channels, NL), "band")
    loss_terms, d_power, d_cross = spectral_terms(
        totals[:channels], totals[channels : 2 * channels], totals[2 * channels :]
    )
    derivative = jnp.pad(
        jnp.stack([d_power, d_cross]),
        ((0, 0), (0, rows - channels), (0, MPAD + width - NL)),
    ).reshape(2 * rows, MPAD + width)
    derivative = lax.dynamic_slice(derivative, (0, first_order), (2 * rows, width))
    inverse_transform = pl.pallas_call(
        functools.partial(synthesise_kernel, rows, width),
        grid=(band_partition,),
        out_shape=jax.ShapeDtypeStruct((band_partition, 2 * rows, lat_count), jnp.bfloat16),
        in_specs=[
            table_spec,
            column_spec,
            pl.BlockSpec((2 * rows, width), lambda i: (0, 0)),
        ],
        out_specs=pl.BlockSpec((1, 2 * rows, lat_count), lambda i: (i, 0, 0)),
        name="synthesise",
    )(tables, padded_columns, derivative)
    inverse_transform = inverse_transform.reshape(band_partition, 2, rows, lat_count)[
        :, :, :channels
    ].reshape(band_partition, 2 * channels, lat_count)
    rows_back = lax.all_to_all(inverse_transform, "band", split_axis=2, concat_axis=0, tiled=True)
    upstream_gradient = jnp.einsum(
        "mqcj,kqm->cjk",
        rows_back.reshape(MPAD, 2, channels, latitude_rows),
        harmonic_basis,
        preferred_element_type=jnp.float32,
    )
    flat_cot = upstream_gradient.astype(jnp.bfloat16).reshape(channels, cell_count)
    weight_part = lax.dot_general(
        flat_cot, flat_latent, (((1,), (1,)), ((), ())), preferred_element_type=jnp.float32
    )
    grad_weight = lax.psum(weight_part, "band") / math.sqrt(cell_count * bands)
    half_width = latent_width // lax.axis_size("chan")
    half_weight = lax.dynamic_slice_in_dim(
        lax.all_gather(decoder_weight, "chan", axis=0, tiled=True),
        lax.axis_index("chan") * half_width,
        half_width,
        1,
    )
    latent_sum = lax.dot_general(
        half_weight,
        lax.all_gather(flat_cot, "chan", axis=0, tiled=True),
        (((0,), (0,)), ((), ())),
        preferred_element_type=jnp.float32,
    )
    grad_latent = latent_sum.astype(jnp.bfloat16).reshape(half_width, latitude_rows, NLON)
    return (grad_latent, grad_weight, loss_terms)


def solution(mesh):
    return jax.shard_map(
        local,
        mesh=mesh,
        in_specs=(P(None, "band", None), P("chan", None), P("chan", "band", None)),
        out_specs=(P("chan", "band", None), P("chan", None), P("chan", None)),
        check_vma=False,
    )
```

```python
import functools
import math

import jax
import jax.numpy as jnp
from jax import lax
from jax.experimental import pallas as pl
from jax.experimental.pallas import tpu as pltpu
from jax.sharding import PartitionSpec as P

NLON = 1440
TRUNC = 720
MPAD = 768
NL = 721
NLP = 768


def fourier_table(order_ids):
    fine_count = 40

    def parts(longitude):
        phase_index = longitude[:, None] * order_ids[None, :] % NLON
        angles = 2.0 * math.pi / NLON * phase_index.astype(jnp.float32)
        return jnp.cos(angles), jnp.sin(angles)

    coarse_cos, coarse_sin = parts(jnp.arange(NLON // fine_count) * fine_count)
    fine_cos, fine_sin = parts(jnp.arange(fine_count))
    scale = jnp.where(order_ids <= TRUNC, 1.0 / math.sqrt(NLON), 0.0)[None, :]
    coarse_cos, coarse_sin, fine_cos, fine_sin = lax.optimization_barrier(
        (coarse_cos * scale, coarse_sin * scale, fine_cos, fine_sin)
    )
    cosines = coarse_cos[:, None] * fine_cos[None] - coarse_sin[:, None] * fine_sin[None]
    sines = coarse_sin[:, None] * fine_cos[None] + coarse_cos[:, None] * fine_sin[None]
    shape = (NLON, order_ids.shape[0])
    basis = jnp.stack([cosines.reshape(shape), -sines.reshape(shape)], axis=1)
    return basis.astype(jnp.bfloat16)


def band_scatter_sum(pieces):
    return jnp.sum(lax.all_to_all(pieces, "band", split_axis=0, concat_axis=0, tiled=True), axis=0)


def band_spread(piece):
    bands = lax.axis_size("band")
    copies = jnp.broadcast_to(piece[None], (bands,) + piece.shape)
    return lax.all_to_all(copies, "band", split_axis=0, concat_axis=0, tiled=True)


def legendre_kernel(cutoff, step_rows, order_ref, start_ref, cos_ref, weight_ref, out_ref, before_ref, current_ref, scale_ref):
    step = pl.program_id(0)

    @pl.when(step == 0)
    def _():
        before_ref[...] = jnp.zeros_like(before_ref)
        current_ref[...] = jnp.ones_like(current_ref)
        scale_ref[...] = start_ref[...]

    order = order_ref[...]
    cosines = cos_ref[...]
    weights = weight_ref[...]
    squared = order * order
    before = before_ref[...]
    current = current_ref[...]
    log_scale = scale_ref[...]
    for row in range(step_rows):
        previous = order + (step * step_rows + row).astype(jnp.float32)
        degree = previous + 1.0
        value = current * jnp.exp(log_scale) * weights
        out_ref[row] = jnp.where(previous <= cutoff, value, 0.0).astype(out_ref.dtype)
        factor = jnp.sqrt((4.0 * degree * degree - 1.0) / (degree * degree - squared))
        back_factor = jnp.sqrt(
            jnp.maximum(previous * previous - squared, 1e-30)
            / jnp.abs(4.0 * previous * previous - 1.0)
        )
        following = factor * (cosines * current - back_factor * before)
        length = current * current + following * following
        inverse = lax.rsqrt(length)
        before = current * inverse
        current = following * inverse
        log_scale = log_scale + 0.5 * jnp.log(length)
    before_ref[...] = before
    current_ref[...] = current
    scale_ref[...] = log_scale


def legendre_rows(order_ids, lat_count, row_total, cutoff):
    lat_index = jnp.arange(lat_count).astype(jnp.float32)
    colatitude = math.pi * (lat_index + 0.5) / lat_count
    cosines = jnp.cos(colatitude)
    colat_sin = jnp.sin(colatitude)
    weights = math.sqrt(math.pi / lat_count) * colat_sin
    order_float = order_ids.astype(jnp.float32)[:, None]
    log_start = (
        0.5 * jnp.log(order_float + 0.5)
        + lax.lgamma(order_float + 0.5)
        - lax.lgamma(order_float + 1.0)
        - 0.5 * math.log(math.pi)
        + order_float * jnp.log(colat_sin)[None, :]
    )
    shape = log_start.shape
    operands = [
        jnp.broadcast_to(order_float, shape),
        log_start,
        jnp.broadcast_to(cosines[None, :], shape),
        jnp.broadcast_to(weights[None, :], shape),
    ]
    step_rows = 16
    return pl.pallas_call(
        functools.partial(legendre_kernel, float(cutoff), step_rows),
        grid=(row_total // step_rows,),
        out_shape=jax.ShapeDtypeStruct((row_total,) + shape, jnp.bfloat16),
        in_specs=[pl.BlockSpec(shape, lambda i: (0, 0))] * 4,
        out_specs=pl.BlockSpec((step_rows,) + shape, lambda i: (i, 0, 0)),
        scratch_shapes=[pltpu.VMEM(shape, jnp.float32)] * 3,
        name="legendre",
    )(*operands)


def analyse_kernel(group, rows, width, table_ref, columns_ref, out_ref):
    step = pl.program_id(0)

    @pl.when(step == 0)
    def _():
        out_ref[...] = jnp.zeros_like(out_ref)

    total = out_ref[...]
    for g in range(group):
        coef = jnp.dot(columns_ref[g], table_ref[g], preferred_element_type=jnp.float32)
        p0, p1, t0, t1 = (coef[i * rows : (i + 1) * rows] for i in range(4))
        spectra = jnp.concatenate(
            [p0 * p0 + p1 * p1, t0 * t0 + t1 * t1, p0 * t0 + p1 * t1], axis=0
        )
        spare = jnp.zeros((3 * rows, width - spectra.shape[1]), jnp.float32)
        total += pltpu.roll(jnp.concatenate([spectra, spare], axis=1), step * group + g, 1)
    out_ref[...] = total


def synthesise_kernel(group, rows, width, table_ref, columns_ref, derivative_ref, out_ref):
    step = pl.program_id(0)
    for g in range(group):
        table = table_ref[g]
        coef = jnp.dot(columns_ref[g], table, preferred_element_type=jnp.float32)
        p0, p1, t0, t1 = (coef[i * rows : (i + 1) * rows] for i in range(4))
        aligned = pltpu.roll(derivative_ref[...], width - (step * group + g), 1)
        aligned = aligned[:, : table.shape[1]]
        d_power, d_cross = 2.0 * aligned[:rows], aligned[rows:]
        gradient = jnp.concatenate(
            [d_power * p0 + d_cross * t0, d_power * p1 + d_cross * t1], axis=0
        )
        out_ref[g] = lax.dot_general(
            gradient.astype(jnp.bfloat16),
            table,
            (((1,), (1,)), ((), ())),
            preferred_element_type=jnp.float32,
        ).astype(out_ref.dtype)


def spectral_terms(power_pred, power_true, cross_power):
    first_power = power_pred + 1.0
    second_power = power_true + 1.0
    first_root = jnp.sqrt(first_power)
    second_root = jnp.sqrt(second_power)
    joint_root = first_root * second_root
    coherence = cross_power / joint_root
    combined = first_power + second_power
    loss_terms = jnp.square(first_root - second_root) + combined * (1.0 - coherence)
    d_power = (
        2.0
        - second_root / first_root
        - coherence
        + combined * cross_power / (2.0 * first_power * joint_root)
    )
    d_cross = -combined / joint_root
    return (loss_terms, d_power, d_cross)


def local(latent, decoder_weight, target):
    bands = lax.axis_size("band")
    band_index = lax.axis_index("band")
    band_partition = MPAD // bands
    latitude_rows = target.shape[1]
    channels = target.shape[0]
    latent_width = latent.shape[0]
    cell_count = latitude_rows * NLON
    slot_ids = jnp.arange(MPAD)
    resident_orders = lax.dynamic_slice_in_dim(
        slot_ids, band_index * band_partition, band_partition, 0
    )
    flat_latent = latent.reshape(latent_width, cell_count)
    predicted = jnp.dot(decoder_weight, flat_latent, preferred_element_type=jnp.float32).astype(
        jnp.bfloat16
    )
    fields = jnp.stack([predicted.reshape(channels, latitude_rows, NLON), target])
    harmonic_basis = fourier_table(slot_ids)
    fourier_modes = jnp.einsum(
        "fclk,kqm->mfqcl", fields, harmonic_basis, preferred_element_type=jnp.float32
    )
    fourier_modes = fourier_modes.astype(jnp.bfloat16).reshape(MPAD, 4 * channels, latitude_rows)
    columns = lax.all_to_all(fourier_modes, "band", split_axis=0, concat_axis=2, tiled=True)
    lat_count = columns.shape[2]
    tables = legendre_rows(resident_orders, lat_count, NLP, TRUNC).transpose(1, 2, 0)
    rows = -(-channels // 8) * 8
    width = NLP + -(-band_partition // 128) * 128
    padded_columns = jnp.pad(
        columns.reshape(band_partition, 4, channels, lat_count),
        ((0, 0), (0, 0), (0, rows - channels), (0, 0)),
    ).reshape(band_partition, 4 * rows, lat_count)
    group = next(g for g in (8, 6, 4, 3, 2, 1) if band_partition % g == 0)
    table_spec = pl.BlockSpec((group, lat_count, NLP), lambda i: (i, 0, 0))
    column_spec = pl.BlockSpec((group, 4 * rows, lat_count), lambda i: (i, 0, 0))
    first_order = band_index * band_partition
    spectra_local = pl.pallas_call(
        functools.partial(analyse_kernel, group, rows, width),
        grid=(band_partition // group,),
        out_shape=jax.ShapeDtypeStruct((3 * rows, width), jnp.float32),
        in_specs=[table_spec, column_spec],
        out_specs=pl.BlockSpec((3 * rows, width), lambda i: (0, 0)),
        name="analyse",
    )(tables, padded_columns)
    by_degree = lax.dynamic_update_slice(
        jnp.zeros((3 * rows, MPAD + width), jnp.float32), spectra_local, (0, first_order)
    )
    pieces = by_degree[:, :MPAD].reshape(3 * rows, bands, band_partition).transpose(1, 0, 2)
    totals = band_scatter_sum(pieces.reshape(bands, 3 * rows * band_partition))
    totals = totals.reshape(3, rows * band_partition)
    terms = jnp.stack(spectral_terms(totals[0], totals[1], totals[2])).reshape(-1)
    terms = band_spread(terms).reshape(bands, 3 * rows, band_partition)
    terms = terms.transpose(1, 0, 2).reshape(3 * rows, MPAD)
    loss_terms = terms[:channels, :NL]
    derivative = jnp.pad(terms[rows:, :NL], ((0, 0), (0, MPAD + width - NL)))
    derivative = lax.dynamic_slice(derivative, (0, first_order), (2 * rows, width))
    inverse_transform = pl.pallas_call(
        functools.partial(synthesise_kernel, group, rows, width),
        grid=(band_partition // group,),
        out_shape=jax.ShapeDtypeStruct((band_partition, 2 * rows, lat_count), jnp.bfloat16),
        in_specs=[
            table_spec,
            column_spec,
            pl.BlockSpec((2 * rows, width), lambda i: (0, 0)),
        ],
        out_specs=pl.BlockSpec((group, 2 * rows, lat_count), lambda i: (i, 0, 0)),
        name="synthesise",
    )(tables, padded_columns, derivative)
    inverse_transform = inverse_transform.reshape(band_partition, 2, rows, lat_count)[
        :, :, :channels
    ].reshape(band_partition, 2 * channels, lat_count)
    rows_back = lax.all_to_all(inverse_transform, "band", split_axis=2, concat_axis=0, tiled=True)
    upstream_gradient = jnp.einsum(
        "mqcj,kqm->cjk",
        rows_back.reshape(MPAD, 2, channels, latitude_rows),
        harmonic_basis,
        preferred_element_type=jnp.float32,
    )
    flat_cot = upstream_gradient.astype(jnp.bfloat16).reshape(channels, cell_count)
    weight_part = lax.dot_general(
        flat_cot, flat_latent, (((1,), (1,)), ((), ())), preferred_element_type=jnp.float32
    )
    weight_size = channels * latent_width
    weight_pad = -weight_size % bands
    weight_pieces = jnp.pad(weight_part.reshape(-1), (0, weight_pad)).reshape(bands, -1)
    weight_sum = band_spread(band_scatter_sum(weight_pieces) / math.sqrt(cell_count * bands))
    grad_weight = weight_sum.reshape(-1)[:weight_size].reshape(channels, latent_width)
    half_width = latent_width // lax.axis_size("chan")
    half_weight = lax.dynamic_slice_in_dim(
        lax.all_gather(decoder_weight, "chan", axis=0, tiled=True),
        lax.axis_index("chan") * half_width,
        half_width,
        1,
    )
    latent_sum = lax.dot_general(
        half_weight,
        lax.all_gather(flat_cot, "chan", axis=0, tiled=True),
        (((0,), (0,)), ((), ())),
        preferred_element_type=jnp.float32,
    )
    grad_latent = latent_sum.astype(jnp.bfloat16).reshape(half_width, latitude_rows, NLON)
    return (grad_latent, grad_weight, loss_terms)


def solution(mesh):
    return jax.shard_map(
        local,
        mesh=mesh,
        in_specs=(P(None, "band", None), P("chan", None), P("chan", "band", None)),
        out_specs=(P("chan", "band", None), P("chan", None), P("chan", None)),
        check_vma=False,
    )
```
